32 devices in a mesh: blk: 4 (over y, core), inner: 8 (over z, x).
Axes of the slice: x: 2, y: 2, z: 4, core: 2. Of those that a mesh axis runs over, the one named last changes fastest.
Arguments:
- queries: bfloat16 [512, 1024], P(('blk', 'inner')), may hold values from -2 to 2
- passages: bfloat16 [512, 1024], P(('blk', 'inner')), may hold values from -2 to 2
- positive: int32 [512], P(('blk', 'inner')), may hold values from 0 to 511, as said below
- query_dups: int32 [512], P(('blk', 'inner')), may hold values from 0 to 127, as said below
- passage_dups: int32 [512], P(('blk', 'inner')), may hold values from 0 to 127, as said below
Outputs:
- query_grad: float32 [512, 1024], P(('blk', 'inner'))
- passage_grad: float32 [512, 1024], P(('blk', 'inner'))
- losses: float32 [512], P(('blk', 'inner'))
The draws below stay inside these ranges and needn't reach their ends.
Inputs may be any that keep to these rules, and one draw needn't show every extreme that they name: Each passage is the positive passage of exactly one query. `query_dups`: a query and a passage, two queries or two passages with equal ids are duplicates of each other. `passage_dups`: ids share one range with query_dups.
All inputs are finite; a program needn't handle non-finite values.
Results may differ from the reference program's by a relative error of at most 0.0026.
Values may be sent and summed in bfloat16 or wider, within the bound.
A program may use at most 64 MiB of HBM per device.

```python
import math
import jax
import jax.numpy as jnp
from jax import lax

D = 1024
NQ = 512
DUP_IDS = 128


def shared_labels(key):
    pairing = jax.random.permutation(jax.random.fold_in(key, 501), jnp.arange(NQ, dtype=jnp.int32))
    query_ids = jax.random.randint(jax.random.fold_in(key, 502), (NQ,), 0, DUP_IDS, dtype=jnp.int32)
    passage_ids = jax.random.randint(jax.random.fold_in(key, 503), (NQ,), 0, DUP_IDS, dtype=jnp.int32)
    spot_index = jax.random.randint(jax.random.fold_in(key, 504), (2,), 0, NQ // 2, dtype=jnp.int32)
    query_ids = query_ids.at[spot_index[0]].set(DUP_IDS - 1).at[spot_index[0] + NQ // 2].set(0)
    passage_ids = passage_ids.at[spot_index[1]].set(DUP_IDS - 1).at[spot_index[1] + NQ // 2].set(0)
    return (pairing, query_ids, passage_ids)


def shared_parts(key):
    anchor = jax.random.normal(jax.random.fold_in(key, 601), (NQ, D), jnp.float32)
    topics = jax.random.normal(jax.random.fold_in(key, 602), (DUP_IDS, D), jnp.float32)
    return (anchor, topics)


def draw_positive(key, part):
    pairing, query_ids, passage_ids = shared_labels(key)
    return pairing


def draw_query_dups(key, part):
    pairing, query_ids, passage_ids = shared_labels(key)
    return query_ids


def draw_passage_dups(key, part):
    pairing, query_ids, passage_ids = shared_labels(key)
    return passage_ids


def draw_queries(key, part):
    pairing, query_ids, passage_ids = shared_labels(key)
    anchor, topics = shared_parts(key)
    key = jax.random.fold_in(key, 11)
    jitter_key = jax.random.fold_in(key, 0)
    jitter = jax.random.normal(jitter_key, (NQ, D), jnp.float32)
    vectors = 0.5 * anchor + 0.7 * topics[query_ids] + jitter
    return jnp.clip(vectors * D ** (-0.5), -2.0, 2.0).astype(jnp.bfloat16)


def draw_passages(key, part):
    pairing, query_ids, passage_ids = shared_labels(key)
    anchor, topics = shared_parts(key)
    key = jax.random.fold_in(key, 12)
    jitter_key = jax.random.fold_in(key, 0)
    owner = jnp.zeros((NQ,), jnp.int32).at[pairing].set(jnp.arange(NQ, dtype=jnp.int32))
    shared_part = 0.5 * anchor[owner] + 0.7 * topics[passage_ids]
    jitter = jax.random.normal(jitter_key, (NQ, D), jnp.float32)
    vectors = shared_part + jitter
    return jnp.clip(vectors * D ** (-0.5), -2.0, 2.0).astype(jnp.bfloat16)


def setup_inputs(seed: int = 0) -> dict:
    splits = jax.random.split(jax.random.key(seed), 6)
    queries = draw_queries(jax.random.fold_in(splits[5], 71), 0)
    passages = draw_passages(jax.random.fold_in(splits[5], 71), 0)
    positive = draw_positive(jax.random.fold_in(splits[5], 71), 0)
    query_dups = draw_query_dups(jax.random.fold_in(splits[5], 71), 0)
    passage_dups = draw_passage_dups(jax.random.fold_in(splits[5], 71), 0)
    return dict(queries=queries, passages=passages, positive=positive, query_dups=query_dups, passage_dups=passage_dups)


SCALE = 50.0
NEGATIVE = -1e30


def pairing_tables(positive, query_dups, passage_dups):
    total_queries = positive.shape[0]
    counter = jnp.arange(total_queries, dtype=jnp.int32)
    inverse = jnp.zeros((total_queries,), jnp.int32).at[positive].set(counter)
    partner = jnp.concatenate([positive.astype(jnp.int32) + total_queries, inverse]).astype(jnp.int32)
    dup_table = jnp.concatenate([query_dups, passage_dups]).astype(jnp.int32)
    return inverse, partner, dup_table


def reference(queries, passages, positive, query_dups, passage_dups):
    inverse, partner, dup_table = pairing_tables(positive, query_dups, passage_dups)
    embedded = jnp.concatenate([queries, passages], 0).astype(jnp.float32)
    row_total = embedded.shape[0]
    total_queries = queries.shape[0]
    block_size = math.gcd(row_total, 512)
    block_count = row_total // block_size
    all_ident = jnp.arange(row_total, dtype=jnp.int32)

    def block_scores(index):
        row_start = (index * block_size).astype(jnp.int32)
        rows_here = lax.dynamic_slice_in_dim(embedded, row_start, block_size, 0)
        scores = SCALE * jnp.dot(rows_here, embedded.T, preferred_element_type=jnp.float32)
        row_ident = row_start + jnp.arange(block_size, dtype=jnp.int32)
        row_dup = lax.dynamic_slice_in_dim(dup_table, row_start, block_size, 0)
        row_partner = lax.dynamic_slice_in_dim(partner, row_start, block_size, 0)
        paired = row_partner[:, None] == all_ident[None, :]
        allowed = (row_ident[:, None] != all_ident[None, :]) & ((row_dup[:, None] != dup_table[None, :]) | paired)
        return row_start, scores, allowed, paired

    def statistics(index):
        row_start, scores, allowed, paired = block_scores(index)
        masked = jnp.where(allowed, scores, NEGATIVE)
        row_top = jnp.max(masked, axis=1)
        row_sum = jnp.sum(jnp.where(allowed, jnp.exp(masked - row_top[:, None]), 0.0), axis=1)
        return row_top + jnp.log(row_sum), jnp.sum(jnp.where(paired, scores, 0.0), axis=1)

    indices = jnp.arange(block_count, dtype=jnp.int32)
    lse_blocks, pos_blocks = lax.map(statistics, indices)
    log_totals = lse_blocks.reshape(-1)
    positive_scores = pos_blocks.reshape(-1)
    lse_query = log_totals[:total_queries]
    lse_passage = log_totals[total_queries:]
    pair_total = jnp.logaddexp(lse_query, lse_passage[positive])
    losses = pair_total - positive_scores[:total_queries]
    row_weight = jnp.concatenate([jnp.exp(lse_query - pair_total), jnp.exp(lse_passage - pair_total[inverse])])

    def gradients(index):
        row_start, scores, allowed, paired = block_scores(index)
        masked = jnp.where(allowed, scores, NEGATIVE)
        row_lse = lax.dynamic_slice_in_dim(log_totals, row_start, block_size, 0)
        row_c = lax.dynamic_slice_in_dim(row_weight, row_start, block_size, 0)
        mixed = row_c[:, None] * jnp.exp(masked - row_lse[:, None]) + row_weight[None, :] * jnp.exp(masked - log_totals[None, :])
        weights = jnp.where(allowed, mixed, 0.0) - paired.astype(jnp.float32)
        weights = lax.optimization_barrier(weights.astype(jnp.bfloat16))
        return SCALE * jnp.dot(weights.astype(jnp.float32), embedded, preferred_element_type=jnp.float32)

    gradient = lax.map(gradients, indices).reshape(row_total, embedded.shape[1])
    return gradient[:total_queries], gradient[total_queries:], losses
```

```python
import functools

import jax
import jax.numpy as jnp
from jax import lax
from jax.experimental import pallas as pl
from jax.experimental.pallas import tpu as pltpu
from jax.sharding import PartitionSpec as P

SCALE = 50.0
NEGATIVE = -1e30


def joined(x, axis, combine):
    everything = jax.tree.map(lambda part: lax.all_gather(part, axis), x)
    initial = jax.tree.map(lambda part: part[0], everything)

    def step(k, so_far):
        return combine(so_far, jax.tree.map(lambda part: part[k], everything))

    return lax.fori_loop(1, lax.axis_size(axis), step, initial)


def pair_labels(blocks, per_device, total_queries, tables):
    all_pos, inverse, query_ids, passage_ids = tables
    local = blocks[:, None] * per_device + jnp.arange(per_device, dtype=jnp.int32)[None, :]
    row_ident = jnp.concatenate([local, local + total_queries], axis=1).reshape(-1)
    row_dup = jnp.concatenate([query_ids[local], passage_ids[local]], axis=1).reshape(-1)
    row_partner = jnp.concatenate([all_pos[local] + total_queries, inverse[local]], axis=1).reshape(
        -1
    )
    return (row_ident, row_dup, row_partner)


def tile_scores(columns, group_rows):
    return SCALE * lax.dot_general(
        columns, group_rows, (((1,), (1,)), ((), ())), preferred_element_type=jnp.float32
    )


def tile_masks(col_labels, row_labels):
    paired = col_labels[0][:, None] == row_labels[2][None, :]
    allowed = (col_labels[0][:, None] != row_labels[0][None, :]) & (
        (col_labels[1][:, None] != row_labels[1][None, :]) | paired
    )
    return (allowed, paired)


def side_stats(scores, allowed, paired, along):
    masked = jnp.where(allowed, scores, NEGATIVE)
    row_top = jnp.max(masked, axis=along)
    row_sum = jnp.sum(
        jnp.where(allowed, jnp.exp(masked - jnp.expand_dims(row_top, along)), 0.0), axis=along
    )
    row_pos = jnp.sum(jnp.where(paired, scores, 0.0), axis=along)
    return (row_top, row_sum, row_pos)


def combine(earlier, later):
    row_top = jnp.maximum(earlier[0], later[0])
    row_sum = earlier[1] * jnp.exp(earlier[0] - row_top) + later[1] * jnp.exp(later[0] - row_top)
    return (row_top, row_sum, earlier[2] + later[2])


def tile_weights(scores, allowed, paired, row_lse, row_c, col_lse, col_c):
    masked = jnp.where(allowed, scores, NEGATIVE)
    mixed = row_c[None, :] * jnp.exp(masked - row_lse[None, :]) + col_c[:, None] * jnp.exp(
        masked - col_lse[:, None]
    )
    return (jnp.where(allowed, mixed, 0.0) - paired.astype(jnp.float32)).astype(jnp.bfloat16)


def body(queries, passages, positive, query_dups, passage_dups):
    per_device = queries.shape[0]
    own_span = 2 * per_device
    blk_count = lax.axis_size("blk")
    inner_count = lax.axis_size("inner")
    blk_here = lax.axis_index("blk")
    inner_here = lax.axis_index("inner")
    own_rows = jnp.concatenate([queries, passages], 0)
    all_pos, query_ids, passage_ids = (
        lax.all_gather(positive, ("blk", "inner"), axis=0, tiled=True),
        lax.all_gather(query_dups, ("blk", "inner"), axis=0, tiled=True),
        lax.all_gather(passage_dups, ("blk", "inner"), axis=0, tiled=True),
    )
    total_queries = all_pos.shape[0]
    counter = jnp.arange(total_queries, dtype=jnp.int32)
    inverse = jnp.zeros((total_queries,), jnp.int32).at[all_pos].set(counter)
    tables = (all_pos, inverse, query_ids, passage_ids)
    group_rows = lax.all_gather(own_rows, "inner", axis=0, tiled=True)
    slot_index = jnp.arange(inner_count, dtype=jnp.int32)
    row_labels = pair_labels(blk_here * inner_count + slot_index, per_device, total_queries, tables)
    own_start = inner_here * own_span
    columns = lax.all_gather(own_rows, "blk", axis=0, tiled=True)
    col_blocks = jnp.arange(blk_count, dtype=jnp.int32) * inner_count + inner_here
    col_labels = pair_labels(col_blocks, per_device, total_queries, tables)
    scores = tile_scores(columns, group_rows)
    allowed, paired = tile_masks(col_labels, row_labels)
    row_stats = side_stats(scores, allowed, paired, 0)
    row_top, row_sum, row_pos = joined((row_stats[0], row_stats[1], row_stats[2]), "inner", combine)
    group_lse = row_top + jnp.log(row_sum)
    every_lse = lax.all_gather(group_lse, "blk", axis=0, tiled=True)
    arranged = every_lse.reshape(blk_count * inner_count, 2, per_device)
    lse_query = arranged[:, 0, :].reshape(-1)
    lse_passage = arranged[:, 1, :].reshape(-1)
    pair_total = jnp.logaddexp(lse_query, lse_passage[all_pos])
    lse_table = jnp.concatenate([lse_query, lse_passage])
    weight_table = jnp.concatenate(
        [jnp.exp(lse_query - pair_total), jnp.exp(lse_passage - pair_total[inverse])]
    )
    own_block = blk_here * inner_count + inner_here
    losses = lax.dynamic_slice_in_dim(
        pair_total, own_block * per_device, per_device
    ) - lax.dynamic_slice_in_dim(row_pos, own_start, per_device)
    weights = tile_weights(
        scores,
        allowed,
        paired,
        lse_table[row_labels[0]],
        weight_table[row_labels[0]],
        lse_table[col_labels[0]],
        weight_table[col_labels[0]],
    )
    gradient = lax.psum_scatter(
        SCALE
        * lax.dot_general(
            weights, columns, (((0,), (0,)), ((), ())), preferred_element_type=jnp.float32
        ),
        "inner",
        scatter_dimension=0,
        tiled=True,
    )
    return (gradient[:per_device], gradient[per_device:], losses)


LANES = 128


def fits_kernel(blk_count, inner_count):
    lines = inner_count // 2
    return blk_count == 4 and inner_count % 2 == 0 and lines & (lines - 1) == 0 and lines <= 8


def swapped(value, distance):
    result = value
    bit = 1
    while bit <= distance:
        if distance & bit:
            result = result + bit - 2 * bit * (lax.div(value, bit) % 2)
        bit *= 2
    return result


def lane_sum(parts):
    total = parts[0]
    for part in parts[1:]:
        total = total + part
    return total


def fused_kernel(
    blk_count,
    inner_count,
    per_device,
    q_ref,
    p_ref,
    pos_ref,
    qd_ref,
    pd_ref,
    qg_ref,
    pg_ref,
    loss_ref,
    rows,
    label_out,
    labels,
    lse_out,
    lses,
    load_sem,
    row_send,
    row_recv,
    label_send,
    label_recv,
    lse_send,
    lse_recv,
):
    device_count = blk_count * inner_count
    span = 2 * per_device
    total_rows = device_count * span
    total_queries = total_rows // 2
    per_lanes = LANES // span
    groups = device_count // per_lanes
    lines = inner_count // 2

    blk = lax.axis_index("blk")
    inner = lax.axis_index("inner")
    core, y = blk % 2, lax.div(blk, 2)
    x, z = inner % 2, lax.div(inner, 2)
    me = blk * inner_count + inner
    sibling = (blk + 1 - 2 * core, inner)
    x_peer = (blk, inner + 1 - 2 * x)
    y_peer = ((1 - y) * 2 + core, inner)

    def block_of(device):
        return device[0] * inner_count + device[1]

    def at_line(device, z_there):
        return (device[0], z_there * 2 + device[1] % 2)

    def whole(block):
        return rows.at[pl.ds(pl.multiple_of(block * span, span), span)]

    def half(block, k):
        start = pl.multiple_of(block * span + k * per_device, per_device)
        return rows.at[pl.ds(start, per_device)]

    loads = [
        pltpu.make_async_copy(q_ref, half(me, 0), load_sem.at[0]),
        pltpu.make_async_copy(p_ref, half(me, 1), load_sem.at[1]),
    ]
    for copy in loads:
        copy.start()

    barrier = pltpu.get_barrier_semaphore()

    def greet(d, carry):
        target = lax.rem(me + d, device_count)
        pl.semaphore_signal(
            barrier,
            inc=1,
            device_id=(lax.div(target, inner_count), lax.rem(target, inner_count)),
            device_id_type=pl.DeviceIdType.MESH,
        )
        return carry

    lax.fori_loop(1, device_count, greet, 0)

    lane = lax.broadcasted_iota(jnp.int32, (1, LANES), 1)
    own_place = lax.div(lane, span) == lax.rem(me, per_lanes)
    lane_here = lax.rem(lane, span)
    code_row = jnp.zeros((1, LANES), jnp.int32)
    dup_row = jnp.zeros((1, LANES), jnp.int32)
    for k in range(per_device):
        code_row = jnp.where(lane_here == k, pos_ref[k], code_row)
        dup_row = jnp.where(lane_here == k, qd_ref[k], dup_row)
        dup_row = jnp.where(lane_here == per_device + k, pd_ref[k], dup_row)
    passage_lane = lane_here >= per_device
    code_row = jnp.where(
        passage_lane, me * per_device + lane_here - per_device + total_queries, code_row
    )
    label_out[0:1, :] = jnp.where(own_place, code_row, 0)
    label_out[1:2, :] = jnp.where(own_place, dup_row, 0)

    pl.semaphore_wait(barrier, device_count - 1)
    for copy in loads:
        copy.wait()

    sent = []

    def send(ref, device, recv):
        copy = pltpu.make_async_remote_copy(
            src_ref=ref,
            dst_ref=ref,
            send_sem=row_send.at[len(sent)],
            recv_sem=recv,
            device_id=device,
            device_id_type=pl.DeviceIdType.MESH,
        )
        copy.start()
        sent.append(copy)

    def arrived(ref, sem):
        pltpu.make_async_copy(ref, ref, sem).wait()

    def spread(block):
        send(whole(block), x_peer, row_recv.at[block, 0])
        send(whole(block), y_peer, row_recv.at[block, 0])

    def to_sibling(block):
        send(whole(block), sibling, row_recv.at[block, 0])

    spread(me)
    for d in range(1, lines):
        send(whole(me), at_line((blk, inner), swapped(z, d)), row_recv.at[me, 0])
    to_sibling(me)

    own_labels = pltpu.make_async_copy(label_out, labels.at[me], label_recv)
    own_labels.start()

    def send_small(out, into, send_sem, recv_sem):
        def step(d, carry):
            target = lax.rem(me + d, device_count)
            pltpu.make_async_remote_copy(
                src_ref=out,
                dst_ref=into.at[me],
                send_sem=send_sem,
                recv_sem=recv_sem,
                device_id=(lax.div(target, inner_count), lax.rem(target, inner_count)),
                device_id_type=pl.DeviceIdType.MESH,
            ).start()
            return carry

        lax.fori_loop(1, device_count, step, 0)

    send_small(label_out, labels, label_send, label_recv)

    for step in range(lines + 2):
        if 1 <= step < lines:
            block = block_of(at_line((blk, inner), swapped(z, step)))
            arrived(whole(block), row_recv.at[block, 0])
            spread(block)
            to_sibling(block)
        if 1 <= step <= lines:
            there = swapped(z, step - 1)
            block = block_of(at_line(x_peer, there))
            arrived(whole(block), row_recv.at[block, 0])
            send(half(block, 0), y_peer, row_recv.at[block, 0])
            to_sibling(block)
            block = block_of(at_line(y_peer, there))
            arrived(whole(block), row_recv.at[block, 0])
            send(half(block, 1), x_peer, row_recv.at[block, 1])
            to_sibling(block)
        if step >= 2:
            block = block_of(at_line((y_peer[0], x_peer[1]), swapped(z, step - 2)))
            arrived(half(block, 0), row_recv.at[block, 0])
            arrived(half(block, 1), row_recv.at[block, 1])
            to_sibling(block)

    arrived(labels, label_recv)
    codes = [
        lane_sum([labels[g * per_lanes + k][0:1, :] for k in range(per_lanes)])
        for g in range(groups)
    ]
    dups = [
        lane_sum([labels[g * per_lanes + k][1:2, :] for k in range(per_lanes)])
        for g in range(groups)
    ]
    code_lanes = jnp.concatenate(codes, axis=1)
    dup_lanes = jnp.concatenate(dups, axis=1)
    partner_lanes = jnp.where(
        code_lanes >= total_queries, code_lanes - total_queries, code_lanes + total_queries
    )
    sub = lax.broadcasted_iota(jnp.int32, (span, LANES), 0)
    lane2 = lax.broadcasted_iota(jnp.int32, (span, LANES), 1)
    diagonal = lane2 == sub + lax.rem(me, per_lanes) * span
    code_col = jnp.sum(jnp.where(diagonal, label_out[0:1, :], 0), axis=1, keepdims=True)
    dup_col = jnp.sum(jnp.where(diagonal, label_out[1:2, :], 0), axis=1, keepdims=True)
    paired = code_col == partner_lanes
    allowed = (code_col != code_lanes) & ((dup_col != dup_lanes) | paired)

    for z_there in range(lines):
        for y_there in range(blk_count // 2):
            for x_there in range(2):
                block = block_of(((2 * y_there + 1 - core), z_there * 2 + x_there))
                arrived(whole(block), row_recv.at[block, 0])

    own = whole(me)[...]
    scores = SCALE * lax.dot_general(
        own, rows[...], (((1,), (1,)), ((), ())), preferred_element_type=jnp.float32
    )
    masked = jnp.where(allowed, scores, NEGATIVE)
    top = jnp.max(masked, axis=1, keepdims=True)
    total = jnp.sum(jnp.where(allowed, jnp.exp(masked - top), 0.0), axis=1, keepdims=True)
    positive_score = jnp.sum(jnp.where(paired, scores, 0.0), axis=1, keepdims=True)
    lse = top + jnp.log(total)
    lse_out[...] = jnp.sum(jnp.where(diagonal, lse, 0.0), axis=0, keepdims=True)

    own_lse = pltpu.make_async_copy(lse_out, lses.at[me], lse_recv)
    own_lse.start()
    send_small(lse_out, lses, lse_send, lse_recv)
    code_cols = jnp.transpose(jnp.concatenate(codes, axis=0))
    arrived(lses, lse_recv)

    lse_rows = [
        lane_sum([lses[g * per_lanes + k] for k in range(per_lanes)]) for g in range(groups)
    ]
    lse_lanes = jnp.concatenate(lse_rows, axis=1)
    lse_cols = jnp.transpose(jnp.concatenate(lse_rows, axis=0))
    found = jnp.zeros((8, total_rows), jnp.float32)
    for g in range(groups):
        match = code_cols[:, g : g + 1] == partner_lanes
        picked = jnp.where(match, lse_cols[:, g : g + 1], 0.0)
        found = found + jnp.sum(picked.reshape(LANES // 8, 8, total_rows), axis=0)
    partner_lse = jnp.sum(found, axis=0, keepdims=True)

    def added(a, b):
        return jnp.maximum(a, b) + jnp.log(1.0 + jnp.exp(-jnp.abs(a - b)))

    pair_lanes = added(lse_lanes, partner_lse)
    pair_col = jnp.sum(jnp.where(paired, pair_lanes, 0.0), axis=1, keepdims=True)
    losses = pair_col - positive_score
    place = lax.broadcasted_iota(jnp.int32, (span, LANES), 0) == lax.broadcasted_iota(
        jnp.int32, (span, LANES), 1
    )
    loss_ref[...] = jnp.sum(jnp.where(place, losses, 0.0), axis=0, keepdims=True)
    mixed = jnp.exp(masked - pair_col) + jnp.exp(masked - pair_lanes)
    weights = jnp.where(allowed, mixed, 0.0) - paired.astype(jnp.float32)
    gradient = SCALE * lax.dot_general(
        weights.astype(jnp.bfloat16),
        rows[...],
        (((1,), (0,)), ((), ())),
        preferred_element_type=jnp.float32,
    )
    qg_ref[...] = gradient[:per_device]
    pg_ref[...] = gradient[per_device:]

    for copy in sent:
        copy.wait_send()
    arrived(labels.at[pl.ds(0, device_count - 1)], label_send)
    arrived(lses.at[pl.ds(0, device_count - 1)], lse_send)


def fused_body(blk_count, inner_count, queries, passages, positive, query_dups, passage_dups):
    per_device, width = queries.shape
    device_count = blk_count * inner_count
    span = 2 * per_device
    sends = (inner_count // 2) * 9 + 8
    vmem = pl.BlockSpec(memory_space=pltpu.VMEM)
    smem = pl.BlockSpec(memory_space=pltpu.SMEM)
    hbm = pl.BlockSpec(memory_space=pl.ANY)
    query_grad, passage_grad, losses = pl.pallas_call(
        functools.partial(fused_kernel, blk_count, inner_count, per_device),
        out_shape=(
            jax.ShapeDtypeStruct((per_device, width), jnp.float32),
            jax.ShapeDtypeStruct((per_device, width), jnp.float32),
            jax.ShapeDtypeStruct((1, LANES), jnp.float32),
        ),
        in_specs=[hbm, hbm, smem, smem, smem],
        out_specs=[vmem, vmem, vmem],
        scratch_shapes=[
            pltpu.VMEM((device_count * span, width), jnp.bfloat16),
            pltpu.VMEM((2, LANES), jnp.int32),
            pltpu.VMEM((device_count, 2, LANES), jnp.int32),
            pltpu.VMEM((1, LANES), jnp.float32),
            pltpu.VMEM((device_count, 1, LANES), jnp.float32),
            pltpu.SemaphoreType.DMA((2,)),
            pltpu.SemaphoreType.DMA((sends,)),
            pltpu.SemaphoreType.DMA((device_count, 2)),
            pltpu.SemaphoreType.DMA,
            pltpu.SemaphoreType.DMA,
            pltpu.SemaphoreType.DMA,
            pltpu.SemaphoreType.DMA,
        ],
        compiler_params=pltpu.CompilerParams(
            collective_id=0, has_side_effects=True, vmem_limit_bytes=32 * 1024 * 1024
        ),
        name="contrastive",
    )(queries, passages, positive, query_dups, passage_dups)
    return query_grad, passage_grad, losses[0, :per_device]


def solution(mesh):
    in_specs = (
        P(("blk", "inner"), None),
        P(("blk", "inner"), None),
        P(("blk", "inner")),
        P(("blk", "inner")),
        P(("blk", "inner")),
    )
    out_specs = (P(("blk", "inner"), None), P(("blk", "inner"), None), P(("blk", "inner")))
    part = body
    blk_count, inner_count = mesh.shape["blk"], mesh.shape["inner"]
    if fits_kernel(blk_count, inner_count):
        part = functools.partial(fused_body, blk_count, inner_count)
    return jax.shard_map(part, mesh=mesh, in_specs=in_specs, out_specs=out_specs, check_vma=False)
```

```python
import functools

import jax
import jax.numpy as jnp
from jax import lax
from jax.experimental import pallas as pl
from jax.experimental.pallas import tpu as pltpu
from jax.sharding import PartitionSpec as P

SCALE = 50.0
NEGATIVE = -1e30


def joined(x, axis, combine):
    everything = jax.tree.map(lambda part: lax.all_gather(part, axis), x)
    initial = jax.tree.map(lambda part: part[0], everything)

    def step(k, so_far):
        return combine(so_far, jax.tree.map(lambda part: part[k], everything))

    return lax.fori_loop(1, lax.axis_size(axis), step, initial)


def pair_labels(blocks, per_device, total_queries, tables):
    all_pos, inverse, query_ids, passage_ids = tables
    local = blocks[:, None] * per_device + jnp.arange(per_device, dtype=jnp.int32)[None, :]
    row_ident = jnp.concatenate([local, local + total_queries], axis=1).reshape(-1)
    row_dup = jnp.concatenate([query_ids[local], passage_ids[local]], axis=1).reshape(-1)
    row_partner = jnp.concatenate([all_pos[local] + total_queries, inverse[local]], axis=1).reshape(
        -1
    )
    return (row_ident, row_dup, row_partner)


def tile_scores(columns, group_rows):
    return SCALE * lax.dot_general(
        columns, group_rows, (((1,), (1,)), ((), ())), preferred_element_type=jnp.float32
    )


def tile_masks(col_labels, row_labels):
    paired = col_labels[0][:, None] == row_labels[2][None, :]
    allowed = (col_labels[0][:, None] != row_labels[0][None, :]) & (
        (col_labels[1][:, None] != row_labels[1][None, :]) | paired
    )
    return (allowed, paired)


def side_stats(scores, allowed, paired, along):
    masked = jnp.where(allowed, scores, NEGATIVE)
    row_top = jnp.max(masked, axis=along)
    row_sum = jnp.sum(
        jnp.where(allowed, jnp.exp(masked - jnp.expand_dims(row_top, along)), 0.0), axis=along
    )
    row_pos = jnp.sum(jnp.where(paired, scores, 0.0), axis=along)
    return (row_top, row_sum, row_pos)


def combine(earlier, later):
    row_top = jnp.maximum(earlier[0], later[0])
    row_sum = earlier[1] * jnp.exp(earlier[0] - row_top) + later[1] * jnp.exp(later[0] - row_top)
    return (row_top, row_sum, earlier[2] + later[2])


def tile_weights(scores, allowed, paired, row_lse, row_c, col_lse, col_c):
    masked = jnp.where(allowed, scores, NEGATIVE)
    mixed = row_c[None, :] * jnp.exp(masked - row_lse[None, :]) + col_c[:, None] * jnp.exp(
        masked - col_lse[:, None]
    )
    return (jnp.where(allowed, mixed, 0.0) - paired.astype(jnp.float32)).astype(jnp.bfloat16)


def body(queries, passages, positive, query_dups, passage_dups):
    per_device = queries.shape[0]
    own_span = 2 * per_device
    blk_count = lax.axis_size("blk")
    inner_count = lax.axis_size("inner")
    blk_here = lax.axis_index("blk")
    inner_here = lax.axis_index("inner")
    own_rows = jnp.concatenate([queries, passages], 0)
    all_pos, query_ids, passage_ids = (
        lax.all_gather(positive, ("blk", "inner"), axis=0, tiled=True),
        lax.all_gather(query_dups, ("blk", "inner"), axis=0, tiled=True),
        lax.all_gather(passage_dups, ("blk", "inner"), axis=0, tiled=True),
    )
    total_queries = all_pos.shape[0]
    counter = jnp.arange(total_queries, dtype=jnp.int32)
    inverse = jnp.zeros((total_queries,), jnp.int32).at[all_pos].set(counter)
    tables = (all_pos, inverse, query_ids, passage_ids)
    group_rows = lax.all_gather(own_rows, "inner", axis=0, tiled=True)
    slot_index = jnp.arange(inner_count, dtype=jnp.int32)
    row_labels = pair_labels(blk_here * inner_count + slot_index, per_device, total_queries, tables)
    own_start = inner_here * own_span
    columns = lax.all_gather(own_rows, "blk", axis=0, tiled=True)
    col_blocks = jnp.arange(blk_count, dtype=jnp.int32) * inner_count + inner_here
    col_labels = pair_labels(col_blocks, per_device, total_queries, tables)
    scores = tile_scores(columns, group_rows)
    allowed, paired = tile_masks(col_labels, row_labels)
    row_stats = side_stats(scores, allowed, paired, 0)
    row_top, row_sum, row_pos = joined((row_stats[0], row_stats[1], row_stats[2]), "inner", combine)
    group_lse = row_top + jnp.log(row_sum)
    every_lse = lax.all_gather(group_lse, "blk", axis=0, tiled=True)
    arranged = every_lse.reshape(blk_count * inner_count, 2, per_device)
    lse_query = arranged[:, 0, :].reshape(-1)
    lse_passage = arranged[:, 1, :].reshape(-1)
    pair_total = jnp.logaddexp(lse_query, lse_passage[all_pos])
    lse_table = jnp.concatenate([lse_query, lse_passage])
    weight_table = jnp.concatenate(
        [jnp.exp(lse_query - pair_total), jnp.exp(lse_passage - pair_total[inverse])]
    )
    own_block = blk_here * inner_count + inner_here
    losses = lax.dynamic_slice_in_dim(
        pair_total, own_block * per_device, per_device
    ) - lax.dynamic_slice_in_dim(row_pos, own_start, per_device)
    weights = tile_weights(
        scores,
        allowed,
        paired,
        lse_table[row_labels[0]],
        weight_table[row_labels[0]],
        lse_table[col_labels[0]],
        weight_table[col_labels[0]],
    )
    gradient = lax.psum_scatter(
        SCALE
        * lax.dot_general(
            weights, columns, (((0,), (0,)), ((), ())), preferred_element_type=jnp.float32
        ),
        "inner",
        scatter_dimension=0,
        tiled=True,
    )
    return (gradient[:per_device], gradient[per_device:], losses)


LANES = 128


def fits_kernel(blk_count, inner_count):
    lines = inner_count // 2
    return blk_count == 4 and inner_count % 2 == 0 and lines & (lines - 1) == 0 and lines <= 8


def swapped(value, distance):
    result = value
    bit = 1
    while bit <= distance:
        if distance & bit:
            result = result + bit - 2 * bit * (lax.div(value, bit) % 2)
        bit *= 2
    return result


def lane_sum(parts):
    total = parts[0]
    for part in parts[1:]:
        total = total + part
    return total


def fused_kernel(
    blk_count,
    inner_count,
    per_device,
    q_ref,
    p_ref,
    label_out,
    qg_ref,
    pg_ref,
    loss_ref,
    scores_ref,
    rows,
    labels,
    lse_out,
    lses,
    row_send,
    row_recv,
    label_send,
    label_recv,
    lse_send,
    lse_recv,
):
    device_count = blk_count * inner_count
    span = 2 * per_device
    total_rows = device_count * span
    total_queries = total_rows // 2
    per_lanes = LANES // span
    groups = device_count // per_lanes
    lines = inner_count // 2

    blk = lax.axis_index("blk")
    inner = lax.axis_index("inner")
    core, y = blk % 2, lax.div(blk, 2)
    x, z = inner % 2, lax.div(inner, 2)
    me = blk * inner_count + inner
    sibling = (blk + 1 - 2 * core, inner)
    x_peer = (blk, inner + 1 - 2 * x)
    y_peer = ((1 - y) * 2 + core, inner)
    diagonal_peer = (y_peer[0], x_peer[1])

    def block_of(device):
        return device[0] * inner_count + device[1]

    def at_line(device, z_there):
        return (device[0], z_there * 2 + device[1] % 2)

    def whole(block):
        return rows.at[pl.ds(pl.multiple_of(block * span, span), span)]

    def half(block, k):
        start = pl.multiple_of(block * span + k * per_device, per_device)
        return rows.at[pl.ds(start, per_device)]

    barrier = pltpu.get_barrier_semaphore()

    def greet(d, carry):
        target = lax.rem(me + d, device_count)
        pl.semaphore_signal(
            barrier,
            inc=1,
            device_id=(lax.div(target, inner_count), lax.rem(target, inner_count)),
            device_id_type=pl.DeviceIdType.MESH,
        )
        return carry

    lax.fori_loop(1, device_count, greet, 0)

    half(me, 0)[...] = q_ref[...]
    half(me, 1)[...] = p_ref[...]
    pl.semaphore_wait(barrier, device_count - 1)
    sent = []

    def send(ref, device, recv):
        copy = pltpu.make_async_remote_copy(
            src_ref=ref,
            dst_ref=ref,
            send_sem=row_send.at[len(sent)],
            recv_sem=recv,
            device_id=device,
            device_id_type=pl.DeviceIdType.MESH,
        )
        copy.start()
        sent.append(copy)

    def arrived(ref, sem):
        pltpu.make_async_copy(ref, ref, sem).wait()

    def spread(block):
        send(whole(block), x_peer, row_recv.at[block, 0])
        send(whole(block), y_peer, row_recv.at[block, 0])

    def send_diagonal(block):
        send(whole(block), diagonal_peer, row_recv.at[block, 0])

    def to_sibling(block):
        send(whole(block), sibling, row_recv.at[block, 0])

    for peer in (x_peer, y_peer):
        send(whole(me), peer, row_recv.at[me, 0])
    for d in range(1, lines):
        send(whole(me), at_line((blk, inner), swapped(z, d)), row_recv.at[me, 0])
    send(whole(me), diagonal_peer, row_recv.at[me, 0])
    send(whole(me), sibling, row_recv.at[me, 0])

    own_label_copy = pltpu.make_async_copy(label_out, labels.at[me], label_recv)
    own_label_copy.start()

    def send_small(out, into, send_sem, recv_sem):
        def step(d, carry):
            target = lax.rem(me + d, device_count)
            pltpu.make_async_remote_copy(
                src_ref=out,
                dst_ref=into.at[me],
                send_sem=send_sem,
                recv_sem=recv_sem,
                device_id=(lax.div(target, inner_count), lax.rem(target, inner_count)),
                device_id_type=pl.DeviceIdType.MESH,
            ).start()
            return carry

        lax.fori_loop(1, device_count, step, 0)

    send_small(label_out, labels, label_send, label_recv)


    forwarded = (1,)
    events = [("line", 1), ("x", 0), ("y", 0)]
    events += [("line", d) for d in range(2, lines)] + [("diagonal", 0)]
    for d in range(1, lines):
        events += [("x", d), ("y", d)] + ([("diagonal", d - 1)] if d > 1 else [])
    events += [("diagonal", lines - 1)]
    for kind, d in events:
        peer = {"line": (blk, inner), "x": x_peer, "y": y_peer, "diagonal": diagonal_peer}[kind]
        block = block_of(at_line(peer, swapped(z, d)))
        if kind == "diagonal" and d in forwarded:
            arrived(half(block, 0), row_recv.at[block, 0])
            arrived(half(block, 1), row_recv.at[block, 1])
        else:
            arrived(whole(block), row_recv.at[block, 0])
        if kind == "line":
            spread(block)
            if d not in forwarded:
                send_diagonal(block)
        if kind == "x" and d in forwarded:
            send(half(block, 0), y_peer, row_recv.at[block, 0])
        if kind == "y" and d in forwarded:
            send(half(block, 1), x_peer, row_recv.at[block, 1])
        to_sibling(block)

    arrived(labels, label_recv)
    codes = [
        lane_sum([labels[g * per_lanes + k][0:1, :] for k in range(per_lanes)])
        for g in range(groups)
    ]
    dups = [
        lane_sum([labels[g * per_lanes + k][1:2, :] for k in range(per_lanes)])
        for g in range(groups)
    ]
    code_lanes = jnp.concatenate(codes, axis=1)
    dup_lanes = jnp.concatenate(dups, axis=1)
    partner_lanes = jnp.where(
        code_lanes >= total_queries, code_lanes - total_queries, code_lanes + total_queries
    )
    sub = lax.broadcasted_iota(jnp.int32, (span, LANES), 0)
    lane2 = lax.broadcasted_iota(jnp.int32, (span, LANES), 1)
    diagonal = lane2 == sub + lax.rem(me, per_lanes) * span
    code_col = jnp.sum(jnp.where(diagonal, label_out[0:1, :], 0), axis=1, keepdims=True)
    dup_col = jnp.sum(jnp.where(diagonal, label_out[1:2, :], 0), axis=1, keepdims=True)
    paired = code_col == partner_lanes
    allowed = (code_col != code_lanes) & ((dup_col != dup_lanes) | paired)

    own = whole(me)[...]
    chunk = inner_count * span
    for part in (blk, sibling[0], y_peer[0], blk_count - 1 - blk):
        if part is not blk and part is not y_peer[0]:
            for there in range(inner_count):
                block = part * inner_count + there
                arrived(whole(block), row_recv.at[block, 0])
        start = pl.multiple_of(part * chunk, chunk)
        scores_ref[:, pl.ds(start, chunk)] = lax.dot_general(
            own,
            rows[pl.ds(start, chunk), :],
            (((1,), (1,)), ((), ())),
            preferred_element_type=jnp.float32,
        )
    scores = SCALE * scores_ref[...]
    masked = jnp.where(allowed, scores, NEGATIVE)
    top = jnp.max(masked, axis=1, keepdims=True)
    total = jnp.sum(jnp.where(allowed, jnp.exp(masked - top), 0.0), axis=1, keepdims=True)
    positive_score = jnp.sum(jnp.where(paired, scores, 0.0), axis=1, keepdims=True)
    lse = top + jnp.log(total)
    lse_out[...] = jnp.sum(jnp.where(diagonal, lse, 0.0), axis=0, keepdims=True)

    own_lse = pltpu.make_async_copy(lse_out, lses.at[me], lse_recv)
    own_lse.start()
    send_small(lse_out, lses, lse_send, lse_recv)
    code_cols = jnp.transpose(jnp.concatenate(codes, axis=0))
    arrived(lses, lse_recv)

    lse_rows = [
        lane_sum([lses[g * per_lanes + k] for k in range(per_lanes)]) for g in range(groups)
    ]
    lse_lanes = jnp.concatenate(lse_rows, axis=1)
    lse_cols = jnp.transpose(jnp.concatenate(lse_rows, axis=0))
    found = jnp.zeros((8, total_rows), jnp.float32)
    for g in range(groups):
        match = code_cols[:, g : g + 1] == partner_lanes
        picked = jnp.where(match, lse_cols[:, g : g + 1], 0.0)
        found = found + jnp.sum(picked.reshape(LANES // 8, 8, total_rows), axis=0)
    partner_lse = jnp.sum(found, axis=0, keepdims=True)

    def added(a, b):
        return jnp.maximum(a, b) + jnp.log(1.0 + jnp.exp(-jnp.abs(a - b)))

    pair_lanes = added(lse_lanes, partner_lse)
    pair_col = jnp.sum(jnp.where(paired, pair_lanes, 0.0), axis=1, keepdims=True)
    losses = pair_col - positive_score
    place = lax.broadcasted_iota(jnp.int32, (span, LANES), 0) == lax.broadcasted_iota(
        jnp.int32, (span, LANES), 1
    )
    loss_ref[...] = jnp.sum(jnp.where(place, losses, 0.0), axis=0, keepdims=True)
    mixed = jnp.exp(masked - pair_col) + jnp.exp(masked - pair_lanes)
    weights = jnp.where(allowed, mixed, 0.0) - paired.astype(jnp.float32)
    gradient = SCALE * lax.dot_general(
        weights.astype(jnp.bfloat16),
        rows[...],
        (((1,), (0,)), ((), ())),
        preferred_element_type=jnp.float32,
    )
    qg_ref[...] = gradient[:per_device]
    pg_ref[...] = gradient[per_device:]

    for copy in sent:
        copy.wait_send()
    arrived(labels.at[pl.ds(0, device_count - 1)], label_send)
    arrived(lses.at[pl.ds(0, device_count - 1)], lse_send)


def label_tile(me, positive, query_dups, passage_dups, total_queries):
    per_device = positive.shape[0]
    span = 2 * per_device
    passages = me * per_device + jnp.arange(per_device, dtype=jnp.int32) + total_queries
    both = jnp.stack(
        [jnp.concatenate([positive, passages]), jnp.concatenate([query_dups, passage_dups])]
    )
    place = jnp.arange(LANES, dtype=jnp.int32) // span == me % (LANES // span)
    return jnp.where(place[None, :], jnp.tile(both, (1, LANES // span)), 0)


def fused_body(blk_count, inner_count, queries, passages, positive, query_dups, passage_dups):
    per_device, width = queries.shape
    device_count = blk_count * inner_count
    span = 2 * per_device
    sends = (inner_count // 2) * 10
    vmem = pl.BlockSpec(memory_space=pltpu.VMEM)
    me = lax.axis_index("blk") * inner_count + lax.axis_index("inner")
    labels = label_tile(me, positive, query_dups, passage_dups, device_count * per_device)
    query_grad, passage_grad, losses = pl.pallas_call(
        functools.partial(fused_kernel, blk_count, inner_count, per_device),
        out_shape=(
            jax.ShapeDtypeStruct((per_device, width), jnp.float32),
            jax.ShapeDtypeStruct((per_device, width), jnp.float32),
            jax.ShapeDtypeStruct((1, LANES), jnp.float32),
        ),
        in_specs=[vmem] * 3,
        out_specs=[vmem, vmem, vmem],
        scratch_shapes=[
            pltpu.VMEM((span, device_count * span), jnp.float32),
            pltpu.VMEM((device_count * span, width), jnp.bfloat16),
            pltpu.VMEM((device_count, 2, LANES), jnp.int32),
            pltpu.VMEM((1, LANES), jnp.float32),
            pltpu.VMEM((device_count, 1, LANES), jnp.float32),
            pltpu.SemaphoreType.DMA((sends,)),
            pltpu.SemaphoreType.DMA((device_count, 2)),
            pltpu.SemaphoreType.DMA,
            pltpu.SemaphoreType.DMA,
            pltpu.SemaphoreType.DMA,
            pltpu.SemaphoreType.DMA,
        ],
        compiler_params=pltpu.CompilerParams(
            collective_id=0, has_side_effects=True, vmem_limit_bytes=32 * 1024 * 1024
        ),
        name="contrastive",
    )(queries, passages, labels)
    return query_grad, passage_grad, losses[0, :per_device]


def solution(mesh):
    in_specs = (
        P(("blk", "inner"), None),
        P(("blk", "inner"), None),
        P(("blk", "inner")),
        P(("blk", "inner")),
        P(("blk", "inner")),
    )
    out_specs = (P(("blk", "inner"), None), P(("blk", "inner"), None), P(("blk", "inner")))
    part = body
    blk_count, inner_count = mesh.shape["blk"], mesh.shape["inner"]
    if fits_kernel(blk_count, inner_count):
        part = functools.partial(fused_body, blk_count, inner_count)
    return jax.shard_map(part, mesh=mesh, in_specs=in_specs, out_specs=out_specs, check_vma=False)
```

```python
import functools

import jax
import jax.numpy as jnp
from jax import lax
from jax.experimental import pallas as pl
from jax.experimental.pallas import tpu as pltpu
from jax.sharding import PartitionSpec as P

SCALE = 50.0
NEGATIVE = -1e30


def joined(x, axis, combine):
    everything = jax.tree.map(lambda part: lax.all_gather(part, axis), x)
    initial = jax.tree.map(lambda part: part[0], everything)

    def step(k, so_far):
        return combine(so_far, jax.tree.map(lambda part: part[k], everything))

    return lax.fori_loop(1, lax.axis_size(axis), step, initial)


def pair_labels(blocks, per_device, total_queries, tables):
    all_pos, inverse, query_ids, passage_ids = tables
    local = blocks[:, None] * per_device + jnp.arange(per_device, dtype=jnp.int32)[None, :]
    row_ident = jnp.concatenate([local, local + total_queries], axis=1).reshape(-1)
    row_dup = jnp.concatenate([query_ids[local], passage_ids[local]], axis=1).reshape(-1)
    row_partner = jnp.concatenate([all_pos[local] + total_queries, inverse[local]], axis=1).reshape(
        -1
    )
    return (row_ident, row_dup, row_partner)


def tile_scores(columns, group_rows):
    return SCALE * lax.dot_general(
        columns, group_rows, (((1,), (1,)), ((), ())), preferred_element_type=jnp.float32
    )


def tile_masks(col_labels, row_labels):
    paired = col_labels[0][:, None] == row_labels[2][None, :]
    allowed = (col_labels[0][:, None] != row_labels[0][None, :]) & (
        (col_labels[1][:, None] != row_labels[1][None, :]) | paired
    )
    return (allowed, paired)


def side_stats(scores, allowed, paired, along):
    masked = jnp.where(allowed, scores, NEGATIVE)
    row_top = jnp.max(masked, axis=along)
    row_sum = jnp.sum(
        jnp.where(allowed, jnp.exp(masked - jnp.expand_dims(row_top, along)), 0.0), axis=along
    )
    row_pos = jnp.sum(jnp.where(paired, scores, 0.0), axis=along)
    return (row_top, row_sum, row_pos)


def combine(earlier, later):
    row_top = jnp.maximum(earlier[0], later[0])
    row_sum = earlier[1] * jnp.exp(earlier[0] - row_top) + later[1] * jnp.exp(later[0] - row_top)
    return (row_top, row_sum, earlier[2] + later[2])


def tile_weights(scores, allowed, paired, row_lse, row_c, col_lse, col_c):
    masked = jnp.where(allowed, scores, NEGATIVE)
    mixed = row_c[None, :] * jnp.exp(masked - row_lse[None, :]) + col_c[:, None] * jnp.exp(
        masked - col_lse[:, None]
    )
    return (jnp.where(allowed, mixed, 0.0) - paired.astype(jnp.float32)).astype(jnp.bfloat16)


def body(queries, passages, positive, query_dups, passage_dups):
    per_device = queries.shape[0]
    own_span = 2 * per_device
    blk_count = lax.axis_size("blk")
    inner_count = lax.axis_size("inner")
    blk_here = lax.axis_index("blk")
    inner_here = lax.axis_index("inner")
    own_rows = jnp.concatenate([queries, passages], 0)
    all_pos, query_ids, passage_ids = (
        lax.all_gather(positive, ("blk", "inner"), axis=0, tiled=True),
        lax.all_gather(query_dups, ("blk", "inner"), axis=0, tiled=True),
        lax.all_gather(passage_dups, ("blk", "inner"), axis=0, tiled=True),
    )
    total_queries = all_pos.shape[0]
    counter = jnp.arange(total_queries, dtype=jnp.int32)
    inverse = jnp.zeros((total_queries,), jnp.int32).at[all_pos].set(counter)
    tables = (all_pos, inverse, query_ids, passage_ids)
    group_rows = lax.all_gather(own_rows, "inner", axis=0, tiled=True)
    slot_index = jnp.arange(inner_count, dtype=jnp.int32)
    row_labels = pair_labels(blk_here * inner_count + slot_index, per_device, total_queries, tables)
    own_start = inner_here * own_span
    columns = lax.all_gather(own_rows, "blk", axis=0, tiled=True)
    col_blocks = jnp.arange(blk_count, dtype=jnp.int32) * inner_count + inner_here
    col_labels = pair_labels(col_blocks, per_device, total_queries, tables)
    scores = tile_scores(columns, group_rows)
    allowed, paired = tile_masks(col_labels, row_labels)
    row_stats = side_stats(scores, allowed, paired, 0)
    row_top, row_sum, row_pos = joined((row_stats[0], row_stats[1], row_stats[2]), "inner", combine)
    group_lse = row_top + jnp.log(row_sum)
    every_lse = lax.all_gather(group_lse, "blk", axis=0, tiled=True)
    arranged = every_lse.reshape(blk_count * inner_count, 2, per_device)
    lse_query = arranged[:, 0, :].reshape(-1)
    lse_passage = arranged[:, 1, :].reshape(-1)
    pair_total = jnp.logaddexp(lse_query, lse_passage[all_pos])
    lse_table = jnp.concatenate([lse_query, lse_passage])
    weight_table = jnp.concatenate(
        [jnp.exp(lse_query - pair_total), jnp.exp(lse_passage - pair_total[inverse])]
    )
    own_block = blk_here * inner_count + inner_here
    losses = lax.dynamic_slice_in_dim(
        pair_total, own_block * per_device, per_device
    ) - lax.dynamic_slice_in_dim(row_pos, own_start, per_device)
    weights = tile_weights(
        scores,
        allowed,
        paired,
        lse_table[row_labels[0]],
        weight_table[row_labels[0]],
        lse_table[col_labels[0]],
        weight_table[col_labels[0]],
    )
    gradient = lax.psum_scatter(
        SCALE
        * lax.dot_general(
            weights, columns, (((0,), (0,)), ((), ())), preferred_element_type=jnp.float32
        ),
        "inner",
        scatter_dimension=0,
        tiled=True,
    )
    return (gradient[:per_device], gradient[per_device:], losses)


LANES = 128


def fits_kernel(blk_count, inner_count):
    lines = inner_count // 2
    return blk_count == 4 and inner_count % 2 == 0 and lines & (lines - 1) == 0 and lines <= 8


def swapped(value, distance):
    result = value
    bit = 1
    while bit <= distance:
        if distance & bit:
            result = result + bit - 2 * bit * (lax.div(value, bit) % 2)
        bit *= 2
    return result


def lane_sum(parts):
    total = parts[0]
    for part in parts[1:]:
        total = total + part
    return total


def fused_kernel(
    blk_count,
    inner_count,
    per_device,
    q_ref,
    p_ref,
    label_out,
    grad_ref,
    loss_ref,
    scores_ref,
    rows,
    labels,
    lse_out,
    lses,
    row_send,
    row_recv,
    label_send,
    label_recv,
    lse_send,
    lse_recv,
):
    device_count = blk_count * inner_count
    span = 2 * per_device
    total_rows = device_count * span
    total_queries = total_rows // 2
    per_lanes = LANES // span
    groups = device_count // per_lanes
    lines = inner_count // 2

    blk = lax.axis_index("blk")
    inner = lax.axis_index("inner")
    core, y = blk % 2, lax.div(blk, 2)
    x, z = inner % 2, lax.div(inner, 2)
    me = blk * inner_count + inner
    sibling = (blk + 1 - 2 * core, inner)
    x_peer = (blk, inner + 1 - 2 * x)
    y_peer = ((1 - y) * 2 + core, inner)
    diagonal_peer = (y_peer[0], x_peer[1])

    def block_of(device):
        return device[0] * inner_count + device[1]

    def at_line(device, z_there):
        return (device[0], z_there * 2 + device[1] % 2)

    def whole(block):
        return rows.at[pl.ds(pl.multiple_of(block * span, span), span)]

    def half(block, k):
        start = pl.multiple_of(block * span + k * per_device, per_device)
        return rows.at[pl.ds(start, per_device)]

    barrier = pltpu.get_barrier_semaphore()

    def greet(d, carry):
        target = lax.rem(me + d, device_count)
        pl.semaphore_signal(
            barrier,
            inc=1,
            device_id=(lax.div(target, inner_count), lax.rem(target, inner_count)),
            device_id_type=pl.DeviceIdType.MESH,
        )
        return carry

    lax.fori_loop(1, device_count, greet, 0)

    half(me, 0)[...] = q_ref[...]
    half(me, 1)[...] = p_ref[...]
    pl.semaphore_wait(barrier, device_count - 1)
    sent = []

    def send(ref, device, recv):
        copy = pltpu.make_async_remote_copy(
            src_ref=ref,
            dst_ref=ref,
            send_sem=row_send.at[len(sent)],
            recv_sem=recv,
            device_id=device,
            device_id_type=pl.DeviceIdType.MESH,
        )
        copy.start()
        sent.append(copy)

    def arrived(ref, sem):
        pltpu.make_async_copy(ref, ref, sem).wait()

    def spread(block):
        send(whole(block), x_peer, row_recv.at[block, 0])
        send(whole(block), y_peer, row_recv.at[block, 0])

    def send_diagonal(block):
        send(whole(block), diagonal_peer, row_recv.at[block, 0])

    def to_sibling(block):
        send(whole(block), sibling, row_recv.at[block, 0])

    for peer in (x_peer, y_peer):
        send(whole(me), peer, row_recv.at[me, 0])
    for d in range(1, lines):
        send(whole(me), at_line((blk, inner), swapped(z, d)), row_recv.at[me, 0])
    send(whole(me), diagonal_peer, row_recv.at[me, 0])
    send(whole(me), sibling, row_recv.at[me, 0])

    own_label_copy = pltpu.make_async_copy(label_out, labels.at[me], label_recv)
    own_label_copy.start()

    def send_small(out, into, send_sem, recv_sem):
        def step(d, carry):
            target = lax.rem(me + d, device_count)
            pltpu.make_async_remote_copy(
                src_ref=out,
                dst_ref=into.at[me],
                send_sem=send_sem,
                recv_sem=recv_sem,
                device_id=(lax.div(target, inner_count), lax.rem(target, inner_count)),
                device_id_type=pl.DeviceIdType.MESH,
            ).start()
            return carry

        lax.fori_loop(1, device_count, step, 0)

    send_small(label_out, labels, label_send, label_recv)


    along_z = [d for d in range(1, lines) if d in (1,3)]
    events = [("line", 1), ("x", 0), ("y", 0), ("diagonal", 0)]
    events += [("line", d) for d in range(2, lines)]
    for d in range(1, lines):
        events += [("x", d), ("y", d), ("diagonal", d)]
    for kind, d in events:
        peer = {"line": (blk, inner), "x": x_peer, "y": y_peer, "diagonal": diagonal_peer}[kind]
        block = block_of(at_line(peer, swapped(z, d)))
        arrived(whole(block), row_recv.at[block, 0])
        if kind == "line":
            spread(block)
            if d not in along_z:
                send_diagonal(block)
        if kind == "diagonal" and d == 0:
            for far in along_z:
                there = at_line((blk, inner), swapped(z, far))
                send(whole(block), there, row_recv.at[block, 0])
        to_sibling(block)

    arrived(labels, label_recv)
    codes = [
        lane_sum([labels[g * per_lanes + k][0:1, :] for k in range(per_lanes)])
        for g in range(groups)
    ]
    dups = [
        lane_sum([labels[g * per_lanes + k][1:2, :] for k in range(per_lanes)])
        for g in range(groups)
    ]
    code_lanes = jnp.concatenate(codes, axis=1)
    dup_lanes = jnp.concatenate(dups, axis=1)
    partner_lanes = jnp.where(
        code_lanes >= total_queries, code_lanes - total_queries, code_lanes + total_queries
    )
    sub = lax.broadcasted_iota(jnp.int32, (span, LANES), 0)
    lane2 = lax.broadcasted_iota(jnp.int32, (span, LANES), 1)
    diagonal = lane2 == sub + lax.rem(me, per_lanes) * span
    code_col = jnp.sum(jnp.where(diagonal, label_out[0:1, :], 0), axis=1, keepdims=True)
    dup_col = jnp.sum(jnp.where(diagonal, label_out[1:2, :], 0), axis=1, keepdims=True)
    paired = code_col == partner_lanes
    allowed = (code_col != code_lanes) & ((dup_col != dup_lanes) | paired)

    own = whole(me)[...]
    chunk = inner_count * span
    for part in (blk, sibling[0], y_peer[0], blk_count - 1 - blk):
        if part is not blk and part is not y_peer[0]:
            for there in range(inner_count):
                block = part * inner_count + there
                arrived(whole(block), row_recv.at[block, 0])
        start = pl.multiple_of(part * chunk, chunk)
        scores_ref[:, pl.ds(start, chunk)] = lax.dot_general(
            own,
            rows[pl.ds(start, chunk), :],
            (((1,), (1,)), ((), ())),
            preferred_element_type=jnp.float32,
        )
    scores = SCALE * scores_ref[...]
    masked = jnp.where(allowed, scores, NEGATIVE)
    top = jnp.max(masked, axis=1, keepdims=True)
    total = jnp.sum(jnp.where(allowed, jnp.exp(masked - top), 0.0), axis=1, keepdims=True)
    positive_score = jnp.sum(jnp.where(paired, scores, 0.0), axis=1, keepdims=True)
    lse = top + jnp.log(total)
    lse_out[...] = jnp.sum(jnp.where(diagonal, lse, 0.0), axis=0, keepdims=True)

    own_lse = pltpu.make_async_copy(lse_out, lses.at[me], lse_recv)
    own_lse.start()
    send_small(lse_out, lses, lse_send, lse_recv)
    code_cols = jnp.transpose(jnp.concatenate(codes, axis=0))
    arrived(lses, lse_recv)

    lse_rows = [
        lane_sum([lses[g * per_lanes + k] for k in range(per_lanes)]) for g in range(groups)
    ]
    lse_lanes = jnp.concatenate(lse_rows, axis=1)
    lse_cols = jnp.transpose(jnp.concatenate(lse_rows, axis=0))
    found = jnp.zeros((8, total_rows), jnp.float32)
    for g in range(groups):
        match = code_cols[:, g : g + 1] == partner_lanes
        picked = jnp.where(match, lse_cols[:, g : g + 1], 0.0)
        found = found + jnp.sum(picked.reshape(LANES // 8, 8, total_rows), axis=0)
    partner_lse = jnp.sum(found, axis=0, keepdims=True)

    def added(a, b):
        return jnp.maximum(a, b) + jnp.log(1.0 + jnp.exp(-jnp.abs(a - b)))

    pair_lanes = added(lse_lanes, partner_lse)
    pair_col = jnp.sum(jnp.where(paired, pair_lanes, 0.0), axis=1, keepdims=True)
    losses = pair_col - positive_score
    place = lax.broadcasted_iota(jnp.int32, (span, LANES), 0) == lax.broadcasted_iota(
        jnp.int32, (span, LANES), 1
    )
    loss_ref[...] = jnp.sum(jnp.where(place, losses, 0.0), axis=0, keepdims=True)
    mixed = jnp.exp(masked - pair_col) + jnp.exp(masked - pair_lanes)
    weights = jnp.where(allowed, mixed, 0.0) - paired.astype(jnp.float32)
    gradient = lax.dot_general(
        weights.astype(jnp.bfloat16),
        rows[...],
        (((1,), (0,)), ((), ())),
        preferred_element_type=jnp.float32,
    )
    grad_ref[...] = gradient

    for copy in sent:
        copy.wait_send()
    arrived(labels.at[pl.ds(0, device_count - 1)], label_send)
    arrived(lses.at[pl.ds(0, device_count - 1)], lse_send)


def label_tile(me, positive, query_dups, passage_dups, total_queries):
    per_device = positive.shape[0]
    span = 2 * per_device
    passages = me * per_device + jnp.arange(per_device, dtype=jnp.int32) + total_queries
    both = jnp.stack(
        [jnp.concatenate([positive, passages]), jnp.concatenate([query_dups, passage_dups])]
    )
    place = jnp.arange(LANES, dtype=jnp.int32) // span == me % (LANES // span)
    return jnp.where(place[None, :], jnp.tile(both, (1, LANES // span)), 0)


def fused_body(blk_count, inner_count, queries, passages, positive, query_dups, passage_dups):
    per_device, width = queries.shape
    device_count = blk_count * inner_count
    span = 2 * per_device
    sends = (inner_count // 2) * 10
    vmem = pl.BlockSpec(memory_space=pltpu.VMEM)
    me = lax.axis_index("blk") * inner_count + lax.axis_index("inner")
    labels = label_tile(me, positive, query_dups, passage_dups, device_count * per_device)
    gradient, losses = pl.pallas_call(
        functools.partial(fused_kernel, blk_count, inner_count, per_device),
        out_shape=(
            jax.ShapeDtypeStruct((span, width), jnp.float32),
            jax.ShapeDtypeStruct((1, LANES), jnp.float32),
        ),
        in_specs=[vmem] * 3,
        out_specs=[vmem, vmem],
        scratch_shapes=[
            pltpu.VMEM((span, device_count * span), jnp.float32),
            pltpu.VMEM((device_count * span, width), jnp.bfloat16),
            pltpu.VMEM((device_count, 2, LANES), jnp.int32),
            pltpu.VMEM((1, LANES), jnp.float32),
            pltpu.VMEM((device_count, 1, LANES), jnp.float32),
            pltpu.SemaphoreType.DMA((sends,)),
            pltpu.SemaphoreType.DMA((device_count, 2)),
            pltpu.SemaphoreType.DMA,
            pltpu.SemaphoreType.DMA,
            pltpu.SemaphoreType.DMA,
            pltpu.SemaphoreType.DMA,
        ],
        compiler_params=pltpu.CompilerParams(
            collective_id=0, has_side_effects=True, vmem_limit_bytes=32 * 1024 * 1024
        ),
        name="contrastive",
    )(queries, passages, labels)
    return SCALE * gradient[:per_device], SCALE * gradient[per_device:], losses[0, :per_device]


def solution(mesh):
    in_specs = (
        P(("blk", "inner"), None),
        P(("blk", "inner"), None),
        P(("blk", "inner")),
        P(("blk", "inner")),
        P(("blk", "inner")),
    )
    out_specs = (P(("blk", "inner"), None), P(("blk", "inner"), None), P(("blk", "inner")))
    part = body
    blk_count, inner_count = mesh.shape["blk"], mesh.shape["inner"]
    if fits_kernel(blk_count, inner_count):
        part = functools.partial(fused_body, blk_count, inner_count)
    return jax.shard_map(part, mesh=mesh, in_specs=in_specs, out_specs=out_specs, check_vma=False)
```

```python
import functools

import jax
import jax.numpy as jnp
from jax import lax
from jax.experimental import pallas as pl
from jax.experimental.pallas import tpu as pltpu
from jax.sharding import PartitionSpec as P

SCALE = 50.0
NEGATIVE = -1e30


def joined(x, axis, combine):
    everything = jax.tree.map(lambda part: lax.all_gather(part, axis), x)
    initial = jax.tree.map(lambda part: part[0], everything)

    def step(k, so_far):
        return combine(so_far, jax.tree.map(lambda part: part[k], everything))

    return lax.fori_loop(1, lax.axis_size(axis), step, initial)


def pair_labels(blocks, per_device, total_queries, tables):
    all_pos, inverse, query_ids, passage_ids = tables
    local = blocks[:, None] * per_device + jnp.arange(per_device, dtype=jnp.int32)[None, :]
    row_ident = jnp.concatenate([local, local + total_queries], axis=1).reshape(-1)
    row_dup = jnp.concatenate([query_ids[local], passage_ids[local]], axis=1).reshape(-1)
    row_partner = jnp.concatenate([all_pos[local] + total_queries, inverse[local]], axis=1).reshape(
        -1
    )
    return (row_ident, row_dup, row_partner)


def tile_scores(columns, group_rows):
    return SCALE * lax.dot_general(
        columns, group_rows, (((1,), (1,)), ((), ())), preferred_element_type=jnp.float32
    )


def tile_masks(col_labels, row_labels):
    paired = col_labels[0][:, None] == row_labels[2][None, :]
    allowed = (col_labels[0][:, None] != row_labels[0][None, :]) & (
        (col_labels[1][:, None] != row_labels[1][None, :]) | paired
    )
    return (allowed, paired)


def side_stats(scores, allowed, paired, along):
    masked = jnp.where(allowed, scores, NEGATIVE)
    row_top = jnp.max(masked, axis=along)
    row_sum = jnp.sum(
        jnp.where(allowed, jnp.exp(masked - jnp.expand_dims(row_top, along)), 0.0), axis=along
    )
    row_pos = jnp.sum(jnp.where(paired, scores, 0.0), axis=along)
    return (row_top, row_sum, row_pos)


def combine(earlier, later):
    row_top = jnp.maximum(earlier[0], later[0])
    row_sum = earlier[1] * jnp.exp(earlier[0] - row_top) + later[1] * jnp.exp(later[0] - row_top)
    return (row_top, row_sum, earlier[2] + later[2])


def tile_weights(scores, allowed, paired, row_lse, row_c, col_lse, col_c):
    masked = jnp.where(allowed, scores, NEGATIVE)
    mixed = row_c[None, :] * jnp.exp(masked - row_lse[None, :]) + col_c[:, None] * jnp.exp(
        masked - col_lse[:, None]
    )
    return (jnp.where(allowed, mixed, 0.0) - paired.astype(jnp.float32)).astype(jnp.bfloat16)


def body(queries, passages, positive, query_dups, passage_dups):
    per_device = queries.shape[0]
    own_span = 2 * per_device
    blk_count = lax.axis_size("blk")
    inner_count = lax.axis_size("inner")
    blk_here = lax.axis_index("blk")
    inner_here = lax.axis_index("inner")
    own_rows = jnp.concatenate([queries, passages], 0)
    all_pos, query_ids, passage_ids = (
        lax.all_gather(positive, ("blk", "inner"), axis=0, tiled=True),
        lax.all_gather(query_dups, ("blk", "inner"), axis=0, tiled=True),
        lax.all_gather(passage_dups, ("blk", "inner"), axis=0, tiled=True),
    )
    total_queries = all_pos.shape[0]
    counter = jnp.arange(total_queries, dtype=jnp.int32)
    inverse = jnp.zeros((total_queries,), jnp.int32).at[all_pos].set(counter)
    tables = (all_pos, inverse, query_ids, passage_ids)
    group_rows = lax.all_gather(own_rows, "inner", axis=0, tiled=True)
    slot_index = jnp.arange(inner_count, dtype=jnp.int32)
    row_labels = pair_labels(blk_here * inner_count + slot_index, per_device, total_queries, tables)
    own_start = inner_here * own_span
    columns = lax.all_gather(own_rows, "blk", axis=0, tiled=True)
    col_blocks = jnp.arange(blk_count, dtype=jnp.int32) * inner_count + inner_here
    col_labels = pair_labels(col_blocks, per_device, total_queries, tables)
    scores = tile_scores(columns, group_rows)
    allowed, paired = tile_masks(col_labels, row_labels)
    row_stats = side_stats(scores, allowed, paired, 0)
    row_top, row_sum, row_pos = joined((row_stats[0], row_stats[1], row_stats[2]), "inner", combine)
    group_lse = row_top + jnp.log(row_sum)
    every_lse = lax.all_gather(group_lse, "blk", axis=0, tiled=True)
    arranged = every_lse.reshape(blk_count * inner_count, 2, per_device)
    lse_query = arranged[:, 0, :].reshape(-1)
    lse_passage = arranged[:, 1, :].reshape(-1)
    pair_total = jnp.logaddexp(lse_query, lse_passage[all_pos])
    lse_table = jnp.concatenate([lse_query, lse_passage])
    weight_table = jnp.concatenate(
        [jnp.exp(lse_query - pair_total), jnp.exp(lse_passage - pair_total[inverse])]
    )
    own_block = blk_here * inner_count + inner_here
    losses = lax.dynamic_slice_in_dim(
        pair_total, own_block * per_device, per_device
    ) - lax.dynamic_slice_in_dim(row_pos, own_start, per_device)
    weights = tile_weights(
        scores,
        allowed,
        paired,
        lse_table[row_labels[0]],
        weight_table[row_labels[0]],
        lse_table[col_labels[0]],
        weight_table[col_labels[0]],
    )
    gradient = lax.psum_scatter(
        SCALE
        * lax.dot_general(
            weights, columns, (((0,), (0,)), ((), ())), preferred_element_type=jnp.float32
        ),
        "inner",
        scatter_dimension=0,
        tiled=True,
    )
    return (gradient[:per_device], gradient[per_device:], losses)


LANES = 128


def fits_kernel(blk_count, inner_count):
    lines = inner_count // 2
    return blk_count == 4 and inner_count % 2 == 0 and lines & (lines - 1) == 0 and lines <= 8


def swapped(value, distance):
    result = value
    bit = 1
    while bit <= distance:
        if distance & bit:
            result = result + bit - 2 * bit * (lax.div(value, bit) % 2)
        bit *= 2
    return result


def lane_sum(parts):
    total = parts[0]
    for part in parts[1:]:
        total = total + part
    return total


def fused_kernel(
    blk_count,
    inner_count,
    per_device,
    q_ref,
    p_ref,
    label_out,
    grad_ref,
    loss_ref,
    scores_ref,
    rows,
    labels,
    lse_out,
    lses,
    row_send,
    row_recv,
    lse_send,
    lse_recv,
):
    device_count = blk_count * inner_count
    span = 2 * per_device
    total_rows = device_count * span
    total_queries = total_rows // 2
    per_lanes = LANES // span
    groups = device_count // per_lanes
    lines = inner_count // 2

    blk = lax.axis_index("blk")
    inner = lax.axis_index("inner")
    core, y = blk % 2, lax.div(blk, 2)
    x, z = inner % 2, lax.div(inner, 2)
    me = blk * inner_count + inner
    sibling = (blk + 1 - 2 * core, inner)
    x_peer = (blk, inner + 1 - 2 * x)
    y_peer = ((1 - y) * 2 + core, inner)
    diagonal_peer = (y_peer[0], x_peer[1])

    def block_of(device):
        return device[0] * inner_count + device[1]

    def at_line(device, z_there):
        return (device[0], z_there * 2 + device[1] % 2)

    def whole(block):
        return rows.at[pl.ds(pl.multiple_of(block * span, span), span)]

    def half(block, k):
        start = pl.multiple_of(block * span + k * per_device, per_device)
        return rows.at[pl.ds(start, per_device)]

    barrier = pltpu.get_barrier_semaphore()

    peers = [x_peer, y_peer, diagonal_peer, sibling]
    peers += [at_line((blk, inner), swapped(z, d)) for d in range(1, lines)]
    for peer in peers:
        pl.semaphore_signal(
            barrier, inc=1, device_id=peer, device_id_type=pl.DeviceIdType.MESH
        )
    labels[me] = label_out[...]
    half(me, 0)[...] = q_ref[...]
    half(me, 1)[...] = p_ref[...]
    pl.semaphore_wait(barrier, len(peers))
    sent = []

    def send(block, device):
        for ref, recv in (
            (labels.at[block], row_recv.at[block, 1]),
            (whole(block), row_recv.at[block, 0]),
        ):
            copy = pltpu.make_async_remote_copy(
                src_ref=ref,
                dst_ref=ref,
                send_sem=row_send.at[len(sent)],
                recv_sem=recv,
                device_id=device,
                device_id_type=pl.DeviceIdType.MESH,
            )
            copy.start()
            sent.append(copy)

    def arrived(ref, sem):
        pltpu.make_async_copy(ref, ref, sem).wait()

    def spread(block):
        send(block, x_peer)
        send(block, y_peer)

    def send_diagonal(block):
        send(block, diagonal_peer)

    def to_sibling(block):
        send(block, sibling)

    for peer in (x_peer, y_peer):
        send(me, peer)
    for d in range(1, lines):
        send(me, at_line((blk, inner), swapped(z, d)))
    send(me, diagonal_peer)
    send(me, sibling)

    def send_small(out, into, send_sem, recv_sem):
        def step(d, carry):
            target = lax.rem(me + d, device_count)
            pltpu.make_async_remote_copy(
                src_ref=out,
                dst_ref=into.at[me],
                send_sem=send_sem,
                recv_sem=recv_sem,
                device_id=(lax.div(target, inner_count), lax.rem(target, inner_count)),
                device_id_type=pl.DeviceIdType.MESH,
            ).start()
            return carry

        lax.fori_loop(1, device_count, step, 0)


    along_z = [d for d in range(1, lines) if d in (1,3)]
    events = [("line", 1), ("x", 0), ("y", 0), ("diagonal", 0)]
    events += [("line", d) for d in range(2, lines)]
    for d in range(1, lines):
        events += [("x", d), ("y", d), ("diagonal", d)]
    for kind, d in events:
        peer = {"line": (blk, inner), "x": x_peer, "y": y_peer, "diagonal": diagonal_peer}[kind]
        block = block_of(at_line(peer, swapped(z, d)))
        arrived(labels.at[block], row_recv.at[block, 1])
        arrived(whole(block), row_recv.at[block, 0])
        if kind == "line":
            spread(block)
            if d not in along_z:
                send_diagonal(block)
        if kind == "diagonal" and d == 0:
            for far in along_z:
                there = at_line((blk, inner), swapped(z, far))
                send(block, there)
        to_sibling(block)

    own = whole(me)[...]
    chunk = inner_count * span
    for part in (blk, sibling[0], y_peer[0], blk_count - 1 - blk):
        if part is not blk and part is not y_peer[0]:
            for there in range(inner_count):
                block = part * inner_count + there
                arrived(labels.at[block], row_recv.at[block, 1])
                arrived(whole(block), row_recv.at[block, 0])
        start = pl.multiple_of(part * chunk, chunk)
        scores_ref[:, pl.ds(start, chunk)] = lax.dot_general(
            own,
            rows[pl.ds(start, chunk), :],
            (((1,), (1,)), ((), ())),
            preferred_element_type=jnp.float32,
        )
    codes = [
        lane_sum([labels[g * per_lanes + k][0:1, :] for k in range(per_lanes)])
        for g in range(groups)
    ]
    dups = [
        lane_sum([labels[g * per_lanes + k][1:2, :] for k in range(per_lanes)])
        for g in range(groups)
    ]
    code_lanes = jnp.concatenate(codes, axis=1)
    dup_lanes = jnp.concatenate(dups, axis=1)
    partner_lanes = jnp.where(
        code_lanes >= total_queries, code_lanes - total_queries, code_lanes + total_queries
    )
    sub = lax.broadcasted_iota(jnp.int32, (span, LANES), 0)
    lane2 = lax.broadcasted_iota(jnp.int32, (span, LANES), 1)
    diagonal = lane2 == sub + lax.rem(me, per_lanes) * span
    code_col = jnp.sum(jnp.where(diagonal, label_out[0:1, :], 0), axis=1, keepdims=True)
    dup_col = jnp.sum(jnp.where(diagonal, label_out[1:2, :], 0), axis=1, keepdims=True)
    paired = code_col == partner_lanes
    allowed = (code_col != code_lanes) & ((dup_col != dup_lanes) | paired)

    scores = SCALE * scores_ref[...]
    masked = jnp.where(allowed, scores, NEGATIVE)
    top = jnp.max(masked, axis=1, keepdims=True)
    total = jnp.sum(jnp.where(allowed, jnp.exp(masked - top), 0.0), axis=1, keepdims=True)
    positive_score = jnp.sum(jnp.where(paired, scores, 0.0), axis=1, keepdims=True)
    lse = top + jnp.log(total)
    lse_out[...] = jnp.sum(jnp.where(diagonal, lse, 0.0), axis=0, keepdims=True)

    own_lse = pltpu.make_async_copy(lse_out, lses.at[me], lse_recv)
    own_lse.start()
    send_small(lse_out, lses, lse_send, lse_recv)
    code_cols = jnp.transpose(jnp.concatenate(codes, axis=0))
    arrived(lses, lse_recv)

    lse_rows = [
        lane_sum([lses[g * per_lanes + k] for k in range(per_lanes)]) for g in range(groups)
    ]
    lse_lanes = jnp.concatenate(lse_rows, axis=1)
    lse_cols = jnp.transpose(jnp.concatenate(lse_rows, axis=0))
    found = jnp.zeros((8, total_rows), jnp.float32)
    for g in range(groups):
        match = code_cols[:, g : g + 1] == partner_lanes
        picked = jnp.where(match, lse_cols[:, g : g + 1], 0.0)
        found = found + jnp.sum(picked.reshape(LANES // 8, 8, total_rows), axis=0)
    partner_lse = jnp.sum(found, axis=0, keepdims=True)

    def added(a, b):
        return jnp.maximum(a, b) + jnp.log(1.0 + jnp.exp(-jnp.abs(a - b)))

    pair_lanes = added(lse_lanes, partner_lse)
    pair_col = jnp.sum(jnp.where(paired, pair_lanes, 0.0), axis=1, keepdims=True)
    losses = pair_col - positive_score
    place = lax.broadcasted_iota(jnp.int32, (span, LANES), 0) == lax.broadcasted_iota(
        jnp.int32, (span, LANES), 1
    )
    loss_ref[...] = jnp.sum(jnp.where(place, losses, 0.0), axis=0, keepdims=True)
    mixed = jnp.exp(masked - pair_col) + jnp.exp(masked - pair_lanes)
    weights = jnp.where(allowed, mixed, 0.0) - paired.astype(jnp.float32)
    gradient = lax.dot_general(
        weights.astype(jnp.bfloat16),
        rows[...],
        (((1,), (0,)), ((), ())),
        preferred_element_type=jnp.float32,
    )
    grad_ref[...] = gradient

    for copy in sent:
        copy.wait_send()
    arrived(lses.at[pl.ds(0, device_count - 1)], lse_send)


def label_tile(me, positive, query_dups, passage_dups, total_queries):
    per_device = positive.shape[0]
    span = 2 * per_device
    passages = me * per_device + jnp.arange(per_device, dtype=jnp.int32) + total_queries
    both = jnp.stack(
        [jnp.concatenate([positive, passages]), jnp.concatenate([query_dups, passage_dups])]
    )
    place = jnp.arange(LANES, dtype=jnp.int32) // span == me % (LANES // span)
    return jnp.where(place[None, :], jnp.tile(both, (1, LANES // span)), 0)


def fused_body(blk_count, inner_count, queries, passages, positive, query_dups, passage_dups):
    per_device, width = queries.shape
    device_count = blk_count * inner_count
    span = 2 * per_device
    sends = (inner_count // 2) * 20
    vmem = pl.BlockSpec(memory_space=pltpu.VMEM)
    me = lax.axis_index("blk") * inner_count + lax.axis_index("inner")
    labels = label_tile(me, positive, query_dups, passage_dups, device_count * per_device)
    gradient, losses = pl.pallas_call(
        functools.partial(fused_kernel, blk_count, inner_count, per_device),
        out_shape=(
            jax.ShapeDtypeStruct((span, width), jnp.float32),
            jax.ShapeDtypeStruct((1, LANES), jnp.float32),
        ),
        in_specs=[vmem] * 3,
        out_specs=[vmem, vmem],
        scratch_shapes=[
            pltpu.VMEM((span, device_count * span), jnp.float32),
            pltpu.VMEM((device_count * span, width), jnp.bfloat16),
            pltpu.VMEM((device_count, 2, LANES), jnp.int32),
            pltpu.VMEM((1, LANES), jnp.float32),
            pltpu.VMEM((device_count, 1, LANES), jnp.float32),
            pltpu.SemaphoreType.DMA((sends,)),
            pltpu.SemaphoreType.DMA((device_count, 2)),
            pltpu.SemaphoreType.DMA,
            pltpu.SemaphoreType.DMA,
        ],
        compiler_params=pltpu.CompilerParams(
            collective_id=0, has_side_effects=True, vmem_limit_bytes=32 * 1024 * 1024
        ),
        name="contrastive",
    )(queries, passages, labels)
    return SCALE * gradient[:per_device], SCALE * gradient[per_device:], losses[0, :per_device]


def solution(mesh):
    in_specs = (
        P(("blk", "inner"), None),
        P(("blk", "inner"), None),
        P(("blk", "inner")),
        P(("blk", "inner")),
        P(("blk", "inner")),
    )
    out_specs = (P(("blk", "inner"), None), P(("blk", "inner"), None), P(("blk", "inner")))
    part = body
    blk_count, inner_count = mesh.shape["blk"], mesh.shape["inner"]
    if fits_kernel(blk_count, inner_count):
        part = functools.partial(fused_body, blk_count, inner_count)
    return jax.shard_map(part, mesh=mesh, in_specs=in_specs, out_specs=out_specs, check_vma=False)
```

```python
import functools

import jax
import jax.numpy as jnp
from jax import lax
from jax.experimental import pallas as pl
from jax.experimental.pallas import tpu as pltpu
from jax.sharding import PartitionSpec as P

SCALE = 50.0
NEGATIVE = -1e30


def joined(x, axis, combine):
    everything = jax.tree.map(lambda part: lax.all_gather(part, axis), x)
    initial = jax.tree.map(lambda part: part[0], everything)

    def step(k, so_far):
        return combine(so_far, jax.tree.map(lambda part: part[k], everything))

    return lax.fori_loop(1, lax.axis_size(axis), step, initial)


def pair_labels(blocks, per_device, total_queries, tables):
    all_pos, inverse, query_ids, passage_ids = tables
    local = blocks[:, None] * per_device + jnp.arange(per_device, dtype=jnp.int32)[None, :]
    row_ident = jnp.concatenate([local, local + total_queries], axis=1).reshape(-1)
    row_dup = jnp.concatenate([query_ids[local], passage_ids[local]], axis=1).reshape(-1)
    row_partner = jnp.concatenate([all_pos[local] + total_queries, inverse[local]], axis=1).reshape(
        -1
    )
    return (row_ident, row_dup, row_partner)


def tile_scores(columns, group_rows):
    return SCALE * lax.dot_general(
        columns, group_rows, (((1,), (1,)), ((), ())), preferred_element_type=jnp.float32
    )


def tile_masks(col_labels, row_labels):
    paired = col_labels[0][:, None] == row_labels[2][None, :]
    allowed = (col_labels[0][:, None] != row_labels[0][None, :]) & (
        (col_labels[1][:, None] != row_labels[1][None, :]) | paired
    )
    return (allowed, paired)


def side_stats(scores, allowed, paired, along):
    masked = jnp.where(allowed, scores, NEGATIVE)
    row_top = jnp.max(masked, axis=along)
    row_sum = jnp.sum(
        jnp.where(allowed, jnp.exp(masked - jnp.expand_dims(row_top, along)), 0.0), axis=along
    )
    row_pos = jnp.sum(jnp.where(paired, scores, 0.0), axis=along)
    return (row_top, row_sum, row_pos)


def combine(earlier, later):
    row_top = jnp.maximum(earlier[0], later[0])
    row_sum = earlier[1] * jnp.exp(earlier[0] - row_top) + later[1] * jnp.exp(later[0] - row_top)
    return (row_top, row_sum, earlier[2] + later[2])


def tile_weights(scores, allowed, paired, row_lse, row_c, col_lse, col_c):
    masked = jnp.where(allowed, scores, NEGATIVE)
    mixed = row_c[None, :] * jnp.exp(masked - row_lse[None, :]) + col_c[:, None] * jnp.exp(
        masked - col_lse[:, None]
    )
    return (jnp.where(allowed, mixed, 0.0) - paired.astype(jnp.float32)).astype(jnp.bfloat16)


def body(queries, passages, positive, query_dups, passage_dups):
    per_device = queries.shape[0]
    own_span = 2 * per_device
    blk_count = lax.axis_size("blk")
    inner_count = lax.axis_size("inner")
    blk_here = lax.axis_index("blk")
    inner_here = lax.axis_index("inner")
    own_rows = jnp.concatenate([queries, passages], 0)
    all_pos, query_ids, passage_ids = (
        lax.all_gather(positive, ("blk", "inner"), axis=0, tiled=True),
        lax.all_gather(query_dups, ("blk", "inner"), axis=0, tiled=True),
        lax.all_gather(passage_dups, ("blk", "inner"), axis=0, tiled=True),
    )
    total_queries = all_pos.shape[0]
    counter = jnp.arange(total_queries, dtype=jnp.int32)
    inverse = jnp.zeros((total_queries,), jnp.int32).at[all_pos].set(counter)
    tables = (all_pos, inverse, query_ids, passage_ids)
    group_rows = lax.all_gather(own_rows, "inner", axis=0, tiled=True)
    slot_index = jnp.arange(inner_count, dtype=jnp.int32)
    row_labels = pair_labels(blk_here * inner_count + slot_index, per_device, total_queries, tables)
    own_start = inner_here * own_span
    columns = lax.all_gather(own_rows, "blk", axis=0, tiled=True)
    col_blocks = jnp.arange(blk_count, dtype=jnp.int32) * inner_count + inner_here
    col_labels = pair_labels(col_blocks, per_device, total_queries, tables)
    scores = tile_scores(columns, group_rows)
    allowed, paired = tile_masks(col_labels, row_labels)
    row_stats = side_stats(scores, allowed, paired, 0)
    row_top, row_sum, row_pos = joined((row_stats[0], row_stats[1], row_stats[2]), "inner", combine)
    group_lse = row_top + jnp.log(row_sum)
    every_lse = lax.all_gather(group_lse, "blk", axis=0, tiled=True)
    arranged = every_lse.reshape(blk_count * inner_count, 2, per_device)
    lse_query = arranged[:, 0, :].reshape(-1)
    lse_passage = arranged[:, 1, :].reshape(-1)
    pair_total = jnp.logaddexp(lse_query, lse_passage[all_pos])
    lse_table = jnp.concatenate([lse_query, lse_passage])
    weight_table = jnp.concatenate(
        [jnp.exp(lse_query - pair_total), jnp.exp(lse_passage - pair_total[inverse])]
    )
    own_block = blk_here * inner_count + inner_here
    losses = lax.dynamic_slice_in_dim(
        pair_total, own_block * per_device, per_device
    ) - lax.dynamic_slice_in_dim(row_pos, own_start, per_device)
    weights = tile_weights(
        scores,
        allowed,
        paired,
        lse_table[row_labels[0]],
        weight_table[row_labels[0]],
        lse_table[col_labels[0]],
        weight_table[col_labels[0]],
    )
    gradient = lax.psum_scatter(
        SCALE
        * lax.dot_general(
            weights, columns, (((0,), (0,)), ((), ())), preferred_element_type=jnp.float32
        ),
        "inner",
        scatter_dimension=0,
        tiled=True,
    )
    return (gradient[:per_device], gradient[per_device:], losses)


LANES = 128


def fits_kernel(blk_count, inner_count):
    lines = inner_count // 2
    return blk_count == 4 and inner_count % 2 == 0 and lines & (lines - 1) == 0 and lines <= 8


def swapped(value, distance):
    result = value
    bit = 1
    while bit <= distance:
        if distance & bit:
            result = result + bit - 2 * bit * (lax.div(value, bit) % 2)
        bit *= 2
    return result


def lane_sum(parts):
    total = parts[0]
    for part in parts[1:]:
        total = total + part
    return total


def fused_kernel(
    blk_count,
    inner_count,
    per_device,
    q_ref,
    p_ref,
    label_out,
    grad_ref,
    loss_ref,
    scores_ref,
    rows,
    labels,
    lse_out,
    lses,
    row_send,
    row_recv,
    lse_send,
    lse_recv,
):
    device_count = blk_count * inner_count
    span = 2 * per_device
    total_rows = device_count * span
    total_queries = total_rows // 2
    per_lanes = LANES // span
    groups = device_count // per_lanes
    lines = inner_count // 2

    blk = lax.axis_index("blk")
    inner = lax.axis_index("inner")
    core, y = blk % 2, lax.div(blk, 2)
    x, z = inner % 2, lax.div(inner, 2)
    me = blk * inner_count + inner
    sibling = (blk + 1 - 2 * core, inner)
    x_peer = (blk, inner + 1 - 2 * x)
    y_peer = ((1 - y) * 2 + core, inner)
    diagonal_peer = (y_peer[0], x_peer[1])

    def block_of(device):
        return device[0] * inner_count + device[1]

    def at_line(device, z_there):
        return (device[0], z_there * 2 + device[1] % 2)

    def whole(block):
        return rows.at[pl.ds(pl.multiple_of(block * span, span), span)]

    def half(block, k):
        start = pl.multiple_of(block * span + k * per_device, per_device)
        return rows.at[pl.ds(start, per_device)]

    barrier = pltpu.get_barrier_semaphore()

    peers = [x_peer, y_peer, diagonal_peer, sibling]
    peers += [at_line((blk, inner), swapped(z, d)) for d in range(1, lines)]
    for peer in peers:
        pl.semaphore_signal(
            barrier, inc=1, device_id=peer, device_id_type=pl.DeviceIdType.MESH
        )
    labels[me] = label_out[...]
    half(me, 0)[...] = q_ref[...]
    half(me, 1)[...] = p_ref[...]
    pl.semaphore_wait(barrier, len(peers))
    sent = []

    def send(block, device):
        for ref, recv in (
            (labels.at[block], row_recv.at[block, 1]),
            (whole(block), row_recv.at[block, 0]),
        ):
            copy = pltpu.make_async_remote_copy(
                src_ref=ref,
                dst_ref=ref,
                send_sem=row_send.at[len(sent)],
                recv_sem=recv,
                device_id=device,
                device_id_type=pl.DeviceIdType.MESH,
            )
            copy.start()
            sent.append(copy)

    def arrived(ref, sem):
        pltpu.make_async_copy(ref, ref, sem).wait()

    def spread(block):
        send(block, x_peer)
        send(block, y_peer)

    def send_diagonal(block):
        send(block, diagonal_peer)

    def to_sibling(block):
        send(block, sibling)

    for peer in (x_peer, y_peer):
        send(me, peer)
    for d in range(1, lines):
        send(me, at_line((blk, inner), swapped(z, d)))
    send(me, diagonal_peer)
    send(me, sibling)

    def send_small(out, into, send_sem, recv_sem):
        def step(d, carry):
            target = lax.rem(me + d, device_count)
            pltpu.make_async_remote_copy(
                src_ref=out,
                dst_ref=into.at[me],
                send_sem=send_sem,
                recv_sem=recv_sem,
                device_id=(lax.div(target, inner_count), lax.rem(target, inner_count)),
                device_id_type=pl.DeviceIdType.MESH,
            ).start()
            return carry

        lax.fori_loop(1, device_count, step, 0)


    along_z = [d for d in range(1, lines) if d in (1,3)]
    events = [("line", 1), ("x", 0), ("y", 0), ("diagonal", 0)]
    events += [("line", d) for d in range(2, lines)]
    for d in range(1, lines):
        events += [("x", d), ("y", d), ("diagonal", d)]
    for kind, d in events:
        peer = {"line": (blk, inner), "x": x_peer, "y": y_peer, "diagonal": diagonal_peer}[kind]
        block = block_of(at_line(peer, swapped(z, d)))
        arrived(labels.at[block], row_recv.at[block, 1])
        arrived(whole(block), row_recv.at[block, 0])
        if kind == "line":
            spread(block)
            if d not in along_z:
                send_diagonal(block)
        if kind == "diagonal" and d == 0:
            for far in along_z:
                there = at_line((blk, inner), swapped(z, far))
                send(block, there)
        to_sibling(block)

    own = whole(me)[...]
    chunk = inner_count * span

    def score_part(part):
        start = pl.multiple_of(part * chunk, chunk)
        scores_ref[:, pl.ds(start, chunk)] = lax.dot_general(
            own,
            rows[pl.ds(start, chunk), :],
            (((1,), (1,)), ((), ())),
            preferred_element_type=jnp.float32,
        )

    score_part(blk)
    score_part(y_peer[0])
    sibling_parts = (sibling[0], blk_count - 1 - blk)
    for part in sibling_parts:
        for there in range(inner_count):
            block = part * inner_count + there
            arrived(labels.at[block], row_recv.at[block, 1])
    codes = [
        lane_sum([labels[g * per_lanes + k][0:1, :] for k in range(per_lanes)])
        for g in range(groups)
    ]
    dups = [
        lane_sum([labels[g * per_lanes + k][1:2, :] for k in range(per_lanes)])
        for g in range(groups)
    ]
    code_lanes = jnp.concatenate(codes, axis=1)
    dup_lanes = jnp.concatenate(dups, axis=1)
    partner_lanes = jnp.where(
        code_lanes >= total_queries, code_lanes - total_queries, code_lanes + total_queries
    )
    sub = lax.broadcasted_iota(jnp.int32, (span, LANES), 0)
    lane2 = lax.broadcasted_iota(jnp.int32, (span, LANES), 1)
    diagonal = lane2 == sub + lax.rem(me, per_lanes) * span
    code_col = jnp.sum(jnp.where(diagonal, label_out[0:1, :], 0), axis=1, keepdims=True)
    dup_col = jnp.sum(jnp.where(diagonal, label_out[1:2, :], 0), axis=1, keepdims=True)
    paired = code_col == partner_lanes
    allowed = (code_col != code_lanes) & ((dup_col != dup_lanes) | paired)

    for part in sibling_parts:
        for there in range(inner_count):
            block = part * inner_count + there
            arrived(whole(block), row_recv.at[block, 0])
        score_part(part)
    scores = SCALE * scores_ref[...]
    masked = jnp.where(allowed, scores, NEGATIVE)
    top = jnp.max(masked, axis=1, keepdims=True)
    total = jnp.sum(jnp.where(allowed, jnp.exp(masked - top), 0.0), axis=1, keepdims=True)
    positive_score = jnp.sum(jnp.where(paired, scores, 0.0), axis=1, keepdims=True)
    lse = top + jnp.log(total)
    lse_out[...] = jnp.sum(jnp.where(diagonal, lse, 0.0), axis=0, keepdims=True)

    own_lse = pltpu.make_async_copy(lse_out, lses.at[me], lse_recv)
    own_lse.start()
    send_small(lse_out, lses, lse_send, lse_recv)
    code_cols = jnp.transpose(jnp.concatenate(codes, axis=0))
    arrived(lses, lse_recv)

    lse_rows = [
        lane_sum([lses[g * per_lanes + k] for k in range(per_lanes)]) for g in range(groups)
    ]
    lse_lanes = jnp.concatenate(lse_rows, axis=1)
    lse_cols = jnp.transpose(jnp.concatenate(lse_rows, axis=0))
    found = jnp.zeros((8, total_rows), jnp.float32)
    for g in range(groups):
        match = code_cols[:, g : g + 1] == partner_lanes
        picked = jnp.where(match, lse_cols[:, g : g + 1], 0.0)
        found = found + jnp.sum(picked.reshape(LANES // 8, 8, total_rows), axis=0)
    partner_lse = jnp.sum(found, axis=0, keepdims=True)

    def added(a, b):
        return jnp.maximum(a, b) + jnp.log(1.0 + jnp.exp(-jnp.abs(a - b)))

    pair_lanes = added(lse_lanes, partner_lse)
    pair_col = jnp.sum(jnp.where(paired, pair_lanes, 0.0), axis=1, keepdims=True)
    losses = pair_col - positive_score
    place = lax.broadcasted_iota(jnp.int32, (span, LANES), 0) == lax.broadcasted_iota(
        jnp.int32, (span, LANES), 1
    )
    loss_ref[...] = jnp.sum(jnp.where(place, losses, 0.0), axis=0, keepdims=True)
    mixed = jnp.exp(masked - pair_col) + jnp.exp(masked - pair_lanes)
    weights = jnp.where(allowed, mixed, 0.0) - paired.astype(jnp.float32)
    gradient = lax.dot_general(
        weights.astype(jnp.bfloat16),
        rows[...],
        (((1,), (0,)), ((), ())),
        preferred_element_type=jnp.float32,
    )
    grad_ref[...] = gradient

    for copy in sent:
        copy.wait_send()
    arrived(lses.at[pl.ds(0, device_count - 1)], lse_send)


def label_tile(me, positive, query_dups, passage_dups, total_queries):
    per_device = positive.shape[0]
    span = 2 * per_device
    passages = me * per_device + jnp.arange(per_device, dtype=jnp.int32) + total_queries
    both = jnp.stack(
        [jnp.concatenate([positive, passages]), jnp.concatenate([query_dups, passage_dups])]
    )
    place = jnp.arange(LANES, dtype=jnp.int32) // span == me % (LANES // span)
    return jnp.where(place[None, :], jnp.tile(both, (1, LANES // span)), 0)


def fused_body(blk_count, inner_count, queries, passages, positive, query_dups, passage_dups):
    per_device, width = queries.shape
    device_count = blk_count * inner_count
    span = 2 * per_device
    sends = (inner_count // 2) * 20
    vmem = pl.BlockSpec(memory_space=pltpu.VMEM)
    me = lax.axis_index("blk") * inner_count + lax.axis_index("inner")
    labels = label_tile(me, positive, query_dups, passage_dups, device_count * per_device)
    gradient, losses = pl.pallas_call(
        functools.partial(fused_kernel, blk_count, inner_count, per_device),
        out_shape=(
            jax.ShapeDtypeStruct((span, width), jnp.float32),
            jax.ShapeDtypeStruct((1, LANES), jnp.float32),
        ),
        in_specs=[vmem] * 3,
        out_specs=[vmem, vmem],
        scratch_shapes=[
            pltpu.VMEM((span, device_count * span), jnp.float32),
            pltpu.VMEM((device_count * span, width), jnp.bfloat16),
            pltpu.VMEM((device_count, 2, LANES), jnp.int32),
            pltpu.VMEM((1, LANES), jnp.float32),
            pltpu.VMEM((device_count, 1, LANES), jnp.float32),
            pltpu.SemaphoreType.DMA((sends,)),
            pltpu.SemaphoreType.DMA((device_count, 2)),
            pltpu.SemaphoreType.DMA,
            pltpu.SemaphoreType.DMA,
        ],
        compiler_params=pltpu.CompilerParams(
            collective_id=0, has_side_effects=True, vmem_limit_bytes=32 * 1024 * 1024
        ),
        name="contrastive",
    )(queries, passages, labels)
    return SCALE * gradient[:per_device], SCALE * gradient[per_device:], losses[0, :per_device]


def solution(mesh):
    in_specs = (
        P(("blk", "inner"), None),
        P(("blk", "inner"), None),
        P(("blk", "inner")),
        P(("blk", "inner")),
        P(("blk", "inner")),
    )
    out_specs = (P(("blk", "inner"), None), P(("blk", "inner"), None), P(("blk", "inner")))
    part = body
    blk_count, inner_count = mesh.shape["blk"], mesh.shape["inner"]
    if fits_kernel(blk_count, inner_count):
        part = functools.partial(fused_body, blk_count, inner_count)
    return jax.shard_map(part, mesh=mesh, in_specs=in_specs, out_specs=out_specs, check_vma=False)
```
